32 devices in a mesh: groups: 2 (over x), loop: 4 (over y, core), bulk: 4 (over z).
Axes of the slice: x: 2, y: 2, z: 4, core: 2. Of those that a mesh axis runs over, the one named last changes fastest.
Arguments:
- tokens: bfloat16 [512, 8192], P(('groups', 'bulk'), 'loop'), parts along dimension 0, may hold values from -6 to 6
- gate_weight: bfloat16 [8192, 26624], P('loop', 'bulk'), may hold values from -0.0625 to 0.0625
- up_weight: bfloat16 [8192, 26624], P('loop', 'bulk'), may hold values from -0.0625 to 0.0625
- down_weight: bfloat16 [26624, 8192], P('bulk', 'loop'), may hold values from -0.0390625 to 0.0390625
Outputs:
- mixed: bfloat16 [512, 8192], P(('groups', 'bulk'), 'loop'), parts along dimension 0
The draws below stay inside these ranges and needn't reach their ends.
There are 2 independent parts, one for each index of `groups`. The reference program is written for one: setup_inputs(seed, part) draws one part's arguments, and reference() takes and returns one part's arrays. A program takes and returns all parts, laid end to end along the dimension named above; an argument that names none is the same for every part. Nothing has to cross between parts.
All inputs are finite; a program needn't handle non-finite values.
Results may differ from the reference program's by a relative error of at most 0.019.
Values may be sent and summed in bfloat16 or wider, within the bound.
A program may use at most 192 MiB of HBM per device.

```python
import jax
import jax.numpy as jnp
from jax import lax

D = 8192
FF = 26624
ROWS = 256
N_LOOP = 4


def steps_of(own_key, shape, split, smallest, high):
    def one(axis_at, blocks):
        draws = jax.random.uniform(jax.random.fold_in(jax.random.fold_in(own_key, 6), axis_at), (blocks,), jnp.float32, smallest / len(split), high / len(split))
        return jnp.repeat(jnp.exp(draws), shape[axis_at] // blocks).reshape((-1,) + (1,) * (len(shape) - axis_at - 1))

    factor_of = one(*split[0])
    for cut in split[1:]:
        factor_of = factor_of * one(*cut)
    return factor_of


def gaussian(own_key, dims, deviation, bound, shards=(), dtype=jnp.bfloat16):
    array = deviation * jax.random.normal(own_key, dims, jnp.float32)
    if shards:
        array = array * steps_of(own_key, dims, shards, -0.22, 0.18)
    return jnp.clip(array, -bound, bound).astype(dtype)


def setup_inputs(seed: int = 0, part: int = 0) -> dict:
    key_list = jax.random.split(jax.random.key(seed), 5)
    own_keys = jax.random.split(jax.random.fold_in(key_list[4], part), 5)
    tokens = gaussian(own_keys[0], (ROWS, D), 1.0, 6.0, ((0, 4), (1, 4)))
    gate_weight = gaussian(key_list[1], (D, FF), D ** -0.5, 0.0625, ((0, 4), (1, 4)))
    up_weight = gaussian(key_list[2], (D, FF), D ** -0.5, 0.0625, ((0, 4), (1, 4)))
    down_weight = gaussian(key_list[3], (FF, D), FF ** -0.5, 0.0390625, ((0, 4), (1, 4)))
    return {"tokens": tokens, "gate_weight": gate_weight, "up_weight": up_weight, "down_weight": down_weight}


def reference(tokens, gate_weight, up_weight, down_weight):
    width = D // N_LOOP

    def accumulate(index, totals):
        start = (index * width).astype(jnp.int32)
        feats = lax.dynamic_slice_in_dim(tokens, start, width, 1)
        gate_rows = lax.dynamic_slice_in_dim(gate_weight, start, width, 0)
        up_rows = lax.dynamic_slice_in_dim(up_weight, start, width, 0)
        gate_part = lax.optimization_barrier(jnp.dot(feats, gate_rows, preferred_element_type=jnp.float32).astype(jnp.bfloat16))
        up_part = lax.optimization_barrier(jnp.dot(feats, up_rows, preferred_element_type=jnp.float32).astype(jnp.bfloat16))
        return (totals[0] + gate_part.astype(jnp.float32), totals[1] + up_part.astype(jnp.float32))

    empty = jnp.zeros((ROWS, FF), jnp.float32)
    gate, up = lax.fori_loop(0, N_LOOP, accumulate, (empty, empty))
    hidden = (jax.nn.silu(gate) * up).astype(jnp.bfloat16)
    return jnp.dot(hidden, down_weight, preferred_element_type=jnp.float32).astype(jnp.bfloat16)
```

```python
import functools

import jax
import jax.numpy as jnp
from jax import lax
from jax.experimental import pallas as pl
from jax.experimental.pallas import tpu as pltpu
from jax.sharding import PartitionSpec as P

MESH = pl.DeviceIdType.MESH
PASSES = 2
CHUNK = 256
SLOTS = 16
WSLOTS = 8
DSLOTS = 8
LAG_SUM, LAG_HID, LAG_FWD, LAG_DOWN = 2, 5, 8, 10


def flip(b, r):
    out, k = b, 1
    while k <= r:
        if r & k:
            out = out + k * (1 - 2 * ((b // k) % 2))
        k *= 2
    return out


def kernel(n_loop, n_bulk, tok, gate_hbm, up_hbm, down_hbm, out,
           x, wg, wu, wd, part, core_rcv, ysum, y_rcv, hid, acc, out_snd, out_rcv,
           wg_sem, wu_sem, wd_sem, tok_send, tok_recv, core_send, core_recv,
           y_send, y_recv, hy_send, hy_recv, hc_send, hc_recv, out_send, out_recv):
    n_y = n_loop // 2
    rb, dl = tok.shape
    ff = gate_hbm.shape[1]
    dout = down_hbm.shape[1]
    steps = ff // CHUNK
    total = PASSES * steps
    per = n_bulk // PASSES
    rows = per * rb
    half = rows // 2
    r = half // n_y

    l = lax.axis_index("loop")
    b = lax.axis_index("bulk")
    y, c = l // 2, l % 2
    sib = y * 2 + (1 - c)
    oc = 1 - c

    def y_to(d):
        return lax.rem(y + d, n_y)

    def y_from(d):
        return lax.rem(y + n_y - d, n_y)

    def gu_copies(g):
        s = lax.rem(g, WSLOTS)
        col = pl.multiple_of(lax.rem(g, steps) * CHUNK, CHUNK)
        return (pltpu.make_async_copy(gate_hbm.at[:, pl.ds(col, CHUNK)], wg.at[s], wg_sem.at[s]),
                pltpu.make_async_copy(up_hbm.at[:, pl.ds(col, CHUNK)], wu.at[s], wu_sem.at[s]))

    def d_copy(g):
        s = lax.rem(g, DSLOTS)
        row = pl.multiple_of(lax.rem(g, steps) * CHUNK, CHUNK)
        return pltpu.make_async_copy(down_hbm.at[pl.ds(row, CHUNK), :], wd.at[s], wd_sem.at[s])

    for g in range(min(WSLOTS, total)):
        for cp in gu_copies(jnp.int32(g)):
            cp.start()
    for g in range(min(DSLOTS, total)):
        d_copy(jnp.int32(g)).start()

    barrier = pltpu.get_barrier_semaphore()
    pl.semaphore_signal(barrier, inc=1, device_id={"loop": sib}, device_id_type=MESH)
    for d in range(1, n_y):
        pl.semaphore_signal(barrier, inc=1, device_id={"loop": y_to(d) * 2 + c}, device_id_type=MESH)
    for q in range(1, n_bulk):
        pl.semaphore_signal(barrier, inc=1, device_id={"bulk": flip(b, q)}, device_id_type=MESH)
    pl.semaphore_wait(barrier, 1 + (n_y - 1) + (n_bulk - 1))

    def tok_copy(q):
        return pltpu.make_async_remote_copy(
            src_ref=tok, dst_ref=x.at[q], send_sem=tok_send.at[q], recv_sem=tok_recv.at[q],
            device_id={"bulk": flip(b, q)}, device_id_type=MESH)

    def core_copy(g):
        s = lax.rem(g, SLOTS)
        return pltpu.make_async_remote_copy(
            src_ref=part.at[s, oc], dst_ref=core_rcv.at[s], send_sem=core_send.at[s],
            recv_sem=core_recv.at[s], device_id={"loop": sib}, device_id_type=MESH)

    def y_copy(g, d):
        s = lax.rem(g, SLOTS)
        return pltpu.make_async_remote_copy(
            src_ref=ysum.at[s, y_to(d)], dst_ref=y_rcv.at[s, d - 1], send_sem=y_send.at[s, d - 1],
            recv_sem=y_recv.at[s, d - 1], device_id={"loop": y_to(d) * 2 + c}, device_id_type=MESH)

    def hy_copy(g, d):
        s = lax.rem(g, SLOTS)
        return pltpu.make_async_remote_copy(
            src_ref=hid.at[s, c, y], dst_ref=hid.at[s, c, y], send_sem=hy_send.at[s, d - 1],
            recv_sem=hy_recv.at[s, d - 1], device_id={"loop": y_to(d) * 2 + c}, device_id_type=MESH)

    def hy_wait(g, d):
        s = lax.rem(g, SLOTS)
        pltpu.make_async_remote_copy(
            src_ref=hid.at[s, c, y], dst_ref=hid.at[s, c, y_from(d)], send_sem=hy_send.at[s, d - 1],
            recv_sem=hy_recv.at[s, d - 1], device_id={"loop": y_to(d) * 2 + c},
            device_id_type=MESH).wait_recv()

    def hc_copy(g, d):
        s = lax.rem(g, SLOTS)
        return pltpu.make_async_remote_copy(
            src_ref=hid.at[s, c, y_from(d)], dst_ref=hid.at[s, c, y_from(d)], send_sem=hc_send.at[s, d],
            recv_sem=hc_recv.at[s, d], device_id={"loop": sib}, device_id_type=MESH)

    def hc_wait(g, d):
        s = lax.rem(g, SLOTS)
        pltpu.make_async_remote_copy(
            src_ref=hid.at[s, c, y_from(d)], dst_ref=hid.at[s, oc, y_from(d)], send_sem=hc_send.at[s, d],
            recv_sem=hc_recv.at[s, d], device_id={"loop": sib}, device_id_type=MESH).wait_recv()

    def out_copy(q):
        return pltpu.make_async_remote_copy(
            src_ref=out_snd.at[q], dst_ref=out_rcv.at[q], send_sem=out_send.at[q],
            recv_sem=out_recv.at[q], device_id={"bulk": flip(b, q)}, device_id_type=MESH)

    for q in range(1, per):
        tok_copy(q).start()
    x[0] = tok[...]
    acc[...] = jnp.zeros_like(acc)
    for q in range(1, per):
        tok_copy(q).wait_recv()
    for q in range(max(per, 1), n_bulk):
        tok_copy(q).start()

    def step(t, carry):
        @pl.when(t < total)
        def _():
            g = t
            p = g // steps
            s, w = lax.rem(g, SLOTS), lax.rem(g, WSLOTS)
            for pp in range(1, PASSES):
                @pl.when(g == pp * steps)
                def _():
                    for q in range(pp * per, (pp + 1) * per):
                        tok_copy(q).wait_recv()
            for cp in gu_copies(g):
                cp.wait()
            rows_x = x[pl.ds(p * per, per)].reshape(rows, dl)
            gp = jnp.dot(rows_x, wg[w], preferred_element_type=jnp.float32)
            part[s, :, :, :CHUNK] = gp.astype(jnp.bfloat16).reshape(2, half, CHUNK)
            up = jnp.dot(rows_x, wu[w], preferred_element_type=jnp.float32)
            part[s, :, :, CHUNK:] = up.astype(jnp.bfloat16).reshape(2, half, CHUNK)
            core_copy(g).start()

            @pl.when(g + WSLOTS < total)
            def _():
                for cp in gu_copies(g + WSLOTS):
                    cp.start()

        @pl.when((t >= LAG_SUM) & (t < total + LAG_SUM))
        def _():
            g = t - LAG_SUM
            s = lax.rem(g, SLOTS)
            core_copy(g).wait_recv()
            both = part[s, c].astype(jnp.float32) + core_rcv[s].astype(jnp.float32)
            ysum[s] = both.astype(jnp.bfloat16).reshape(n_y, r, 2 * CHUNK)
            for d in range(1, n_y):
                y_copy(g, d).start()

        @pl.when((t >= LAG_HID) & (t < total + LAG_HID))
        def _():
            g = t - LAG_HID
            s = lax.rem(g, SLOTS)
            tot = ysum[s, y].astype(jnp.float32)
            for d in range(1, n_y):
                y_copy(g, d).wait_recv()
                tot = tot + y_rcv[s, d - 1].astype(jnp.float32)
            gate, up = tot[:, :CHUNK], tot[:, CHUNK:]
            hid[s, c, y] = (gate / (1.0 + jnp.exp(-gate)) * up).astype(jnp.bfloat16)
            for d in range(1, n_y):
                hy_copy(g, d).start()
            hc_copy(g, 0).start()

        @pl.when((t >= LAG_FWD) & (t < total + LAG_FWD))
        def _():
            g = t - LAG_FWD
            for d in range(1, n_y):
                hy_wait(g, d)
                hc_copy(g, d).start()

        @pl.when(t >= LAG_DOWN)
        def _():
            g = t - LAG_DOWN
            p = g // steps
            s, w = lax.rem(g, SLOTS), lax.rem(g, DSLOTS)
            for d in range(n_y):
                hc_wait(g, d)
            d_copy(g).wait()
            acc[p] += jnp.dot(hid[s].reshape(rows, CHUNK), wd[w], preferred_element_type=jnp.float32)
            core_copy(g).wait_send()
            for d in range(1, n_y):
                y_copy(g, d).wait_send()
                hy_copy(g, d).wait_send()
            for d in range(n_y):
                hc_copy(g, d).wait_send()

            @pl.when(g + DSLOTS < total)
            def _():
                d_copy(g + DSLOTS).start()

            for pp in range(PASSES):
                @pl.when(g == pp * steps + steps - 1)
                def _():
                    for q in reversed(range(max(pp * per, 1), (pp + 1) * per)):
                        k = q - pp * per
                        out_snd[q] = acc[pp, k * rb:(k + 1) * rb].astype(jnp.bfloat16)
                        out_copy(q).start()
        return carry

    lax.fori_loop(0, total + LAG_DOWN, step, 0)

    res = acc[0, 0:rb]
    for q in range(1, n_bulk):
        out_copy(q).wait_recv()
        res = res + out_rcv[q].astype(jnp.float32)
    out[...] = res.astype(out.dtype)
    for q in range(1, n_bulk):
        tok_copy(q).wait_send()
        out_copy(q).wait_send()


def body(n_loop, n_bulk, tokens, gate_weight, up_weight, down_weight):
    rb, dl = tokens.shape
    ff, dout = down_weight.shape
    n_y = n_loop // 2
    rows = n_bulk // PASSES * rb
    half = rows // 2
    r = half // n_y
    bf, f32 = jnp.bfloat16, jnp.float32
    dma = pltpu.SemaphoreType.DMA
    vmem = pl.BlockSpec(memory_space=pltpu.VMEM)
    hbm = pl.BlockSpec(memory_space=pl.ANY)
    ny1 = max(n_y - 1, 1)
    return pl.pallas_call(
        functools.partial(kernel, n_loop, n_bulk),
        out_shape=jax.ShapeDtypeStruct((rb, dout), bf),
        in_specs=[vmem, hbm, hbm, hbm],
        out_specs=vmem,
        scratch_shapes=[
            pltpu.VMEM((n_bulk, rb, dl), bf),
            pltpu.VMEM((WSLOTS, dl, CHUNK), bf),
            pltpu.VMEM((WSLOTS, dl, CHUNK), bf),
            pltpu.VMEM((DSLOTS, CHUNK, dout), bf),
            pltpu.VMEM((SLOTS, 2, half, 2 * CHUNK), bf),
            pltpu.VMEM((SLOTS, half, 2 * CHUNK), bf),
            pltpu.VMEM((SLOTS, n_y, r, 2 * CHUNK), bf),
            pltpu.VMEM((SLOTS, ny1, r, 2 * CHUNK), bf),
            pltpu.VMEM((SLOTS, 2, n_y, r, CHUNK), bf),
            pltpu.VMEM((PASSES, rows, dout), f32),
            pltpu.VMEM((n_bulk, rb, dout), bf),
            pltpu.VMEM((n_bulk, rb, dout), bf),
            dma((WSLOTS,)), dma((WSLOTS,)), dma((DSLOTS,)),
            dma((n_bulk,)), dma((n_bulk,)),
            dma((SLOTS,)), dma((SLOTS,)),
            dma((SLOTS, ny1)), dma((SLOTS, ny1)),
            dma((SLOTS, ny1)), dma((SLOTS, ny1)),
            dma((SLOTS, n_y)), dma((SLOTS, n_y)),
            dma((n_bulk,)), dma((n_bulk,)),
        ],
        compiler_params=pltpu.CompilerParams(
            collective_id=0, has_side_effects=True, vmem_limit_bytes=58 * 1024 * 1024),
    )(tokens, gate_weight, up_weight, down_weight)


def solution(mesh):
    return jax.shard_map(
        functools.partial(body, mesh.shape["loop"], mesh.shape["bulk"]),
        mesh=mesh,
        in_specs=(
            P(("groups", "bulk"), "loop"),
            P("loop", "bulk"),
            P("loop", "bulk"),
            P("bulk", "loop"),
        ),
        out_specs=P(("groups", "bulk"), "loop"),
        check_vma=False,
    )
```

```python
import functools

import jax
import jax.numpy as jnp
from jax import lax
from jax.experimental import pallas as pl
from jax.experimental.pallas import tpu as pltpu
from jax.sharding import PartitionSpec as P

MESH = pl.DeviceIdType.MESH
PASSES = 2
CHUNK = 512
SLOTS = 16
WSLOTS = 4
DSLOTS = 4
PIECES = 4
LAGS = (1, 4, 7, 8)
LAG_SUM, LAG_HID, LAG_FWD, LAG_DOWN = LAGS


def flip(b, r):
    out, k = b, 1
    while k <= r:
        if r & k:
            out = out + k * (1 - 2 * ((b // k) % 2))
        k *= 2
    return out


def kernel(n_loop, n_bulk, tok, gate_hbm, up_hbm, down_hbm, out,
           x, wg, wu, wd, part, core_rcv, ysum, y_rcv, hid, acc, out_snd, out_mid, out_rcv,
           wg_sem, wu_sem, wd_sem, tok_send, tok_recv, core_send, core_recv,
           y_send, y_recv, hy_send, hy_recv, hc_send, hc_recv, mid_send, mid_recv, out_send, out_recv):
    n_y = n_loop // 2
    rb, dl = tok.shape
    ff = gate_hbm.shape[1]
    dout = down_hbm.shape[1]
    wp = dout // PIECES
    steps = ff // CHUNK
    total = PASSES * steps
    per = n_bulk // PASSES
    rows = per * rb
    half = rows // 2
    r = half // n_y

    l = lax.axis_index("loop")
    b = lax.axis_index("bulk")
    y, c = l // 2, l % 2
    sib = y * 2 + (1 - c)
    oc = 1 - c

    def y_to(d):
        return lax.rem(y + d, n_y)

    def y_from(d):
        return lax.rem(y + n_y - d, n_y)

    def gu_copies(g):
        s = lax.rem(g, WSLOTS)
        col = pl.multiple_of(lax.rem(g, steps) * CHUNK, CHUNK)
        return (pltpu.make_async_copy(gate_hbm.at[:, pl.ds(col, CHUNK)], wg.at[s], wg_sem.at[s]),
                pltpu.make_async_copy(up_hbm.at[:, pl.ds(col, CHUNK)], wu.at[s], wu_sem.at[s]))

    def d_copy(g):
        s = lax.rem(g, DSLOTS)
        row = pl.multiple_of(lax.rem(g, steps) * CHUNK, CHUNK)
        return pltpu.make_async_copy(down_hbm.at[pl.ds(row, CHUNK), :], wd.at[s], wd_sem.at[s])

    for g in range(min(WSLOTS, total)):
        for cp in gu_copies(jnp.int32(g)):
            cp.start()
    for g in range(min(DSLOTS, total)):
        d_copy(jnp.int32(g)).start()

    barrier = pltpu.get_barrier_semaphore()
    pl.semaphore_signal(barrier, inc=1, device_id={"loop": sib}, device_id_type=MESH)
    for d in range(1, n_y):
        pl.semaphore_signal(barrier, inc=1, device_id={"loop": y_to(d) * 2 + c}, device_id_type=MESH)
    for q in range(1, n_bulk):
        pl.semaphore_signal(barrier, inc=1, device_id={"bulk": flip(b, q)}, device_id_type=MESH)
    pl.semaphore_wait(barrier, 1 + (n_y - 1) + (n_bulk - 1))

    def tok_copy(q):
        return pltpu.make_async_remote_copy(
            src_ref=tok, dst_ref=x.at[q], send_sem=tok_send.at[q], recv_sem=tok_recv.at[q],
            device_id={"bulk": flip(b, q)}, device_id_type=MESH)

    def core_copy(g):
        s = lax.rem(g, SLOTS)
        return pltpu.make_async_remote_copy(
            src_ref=part.at[s, oc], dst_ref=core_rcv.at[s], send_sem=core_send.at[s],
            recv_sem=core_recv.at[s], device_id={"loop": sib}, device_id_type=MESH)

    def y_copy(g, d):
        s = lax.rem(g, SLOTS)
        return pltpu.make_async_remote_copy(
            src_ref=ysum.at[s, y_to(d)], dst_ref=y_rcv.at[s, d - 1], send_sem=y_send.at[s, d - 1],
            recv_sem=y_recv.at[s, d - 1], device_id={"loop": y_to(d) * 2 + c}, device_id_type=MESH)

    def hy_copy(g, d):
        s = lax.rem(g, SLOTS)
        return pltpu.make_async_remote_copy(
            src_ref=hid.at[s, c, y], dst_ref=hid.at[s, c, y], send_sem=hy_send.at[s, d - 1],
            recv_sem=hy_recv.at[s, d - 1], device_id={"loop": y_to(d) * 2 + c}, device_id_type=MESH)

    def hy_wait(g, d):
        s = lax.rem(g, SLOTS)
        pltpu.make_async_remote_copy(
            src_ref=hid.at[s, c, y], dst_ref=hid.at[s, c, y_from(d)], send_sem=hy_send.at[s, d - 1],
            recv_sem=hy_recv.at[s, d - 1], device_id={"loop": y_to(d) * 2 + c},
            device_id_type=MESH).wait_recv()

    def hc_copy(g, d):
        s = lax.rem(g, SLOTS)
        return pltpu.make_async_remote_copy(
            src_ref=hid.at[s, c, y_from(d)], dst_ref=hid.at[s, c, y_from(d)], send_sem=hc_send.at[s, d],
            recv_sem=hc_recv.at[s, d], device_id={"loop": sib}, device_id_type=MESH)

    def hc_wait(g, d):
        s = lax.rem(g, SLOTS)
        pltpu.make_async_remote_copy(
            src_ref=hid.at[s, c, y_from(d)], dst_ref=hid.at[s, oc, y_from(d)], send_sem=hc_send.at[s, d],
            recv_sem=hc_recv.at[s, d], device_id={"loop": sib}, device_id_type=MESH).wait_recv()

    def mid_copy(q, k):
        return pltpu.make_async_remote_copy(
            src_ref=out_snd.at[q, k], dst_ref=out_mid.at[q // 2, k], send_sem=mid_send.at[q // 2, k],
            recv_sem=mid_recv.at[q // 2, k], device_id={"bulk": flip(b, 1)}, device_id_type=MESH)

    def out_copy(q, k):
        return pltpu.make_async_remote_copy(
            src_ref=out_snd.at[q, k], dst_ref=out_rcv.at[q // 2, k], send_sem=out_send.at[q // 2, k],
            recv_sem=out_recv.at[q // 2, k], device_id={"bulk": flip(b, q)}, device_id_type=MESH)

    for q in range(1, per):
        tok_copy(q).start()
    x[0] = tok[...]
    acc[...] = jnp.zeros_like(acc)
    for q in range(1, per):
        tok_copy(q).wait_recv()
    for q in range(max(per, 1), n_bulk):
        tok_copy(q).start()

    def step(t, carry):
        @pl.when(t < total)
        def _():
            g = t
            p = g // steps
            s, w = lax.rem(g, SLOTS), lax.rem(g, WSLOTS)
            for pp in range(1, PASSES):
                @pl.when(g == pp * steps)
                def _():
                    for q in range(pp * per, (pp + 1) * per):
                        tok_copy(q).wait_recv()
            for cp in gu_copies(g):
                cp.wait()
            rows_x = x[pl.ds(p * per, per)].reshape(rows, dl)
            gp = jnp.dot(rows_x, wg[w], preferred_element_type=jnp.float32)
            part[s, :, :, :CHUNK] = gp.astype(jnp.bfloat16).reshape(2, half, CHUNK)
            up = jnp.dot(rows_x, wu[w], preferred_element_type=jnp.float32)
            part[s, :, :, CHUNK:] = up.astype(jnp.bfloat16).reshape(2, half, CHUNK)
            core_copy(g).start()

            @pl.when(g + WSLOTS < total)
            def _():
                for cp in gu_copies(g + WSLOTS):
                    cp.start()

        @pl.when((t >= LAG_SUM) & (t < total + LAG_SUM))
        def _():
            g = t - LAG_SUM
            s = lax.rem(g, SLOTS)
            core_copy(g).wait_recv()
            both = part[s, c].astype(jnp.float32) + core_rcv[s].astype(jnp.float32)
            ysum[s] = both.astype(jnp.bfloat16).reshape(n_y, r, 2 * CHUNK)
            for d in range(1, n_y):
                y_copy(g, d).start()

        @pl.when((t >= LAG_HID) & (t < total + LAG_HID))
        def _():
            g = t - LAG_HID
            s = lax.rem(g, SLOTS)
            tot = ysum[s, y].astype(jnp.float32)
            for d in range(1, n_y):
                y_copy(g, d).wait_recv()
                tot = tot + y_rcv[s, d - 1].astype(jnp.float32)
            gate, up = tot[:, :CHUNK], tot[:, CHUNK:]
            hid[s, c, y] = (gate / (1.0 + jnp.exp(-gate)) * up).astype(jnp.bfloat16)
            for d in range(1, n_y):
                hy_copy(g, d).start()
            hc_copy(g, 0).start()

        @pl.when((t >= LAG_FWD) & (t < total + LAG_FWD))
        def _():
            g = t - LAG_FWD
            for d in range(1, n_y):
                hy_wait(g, d)
                hc_copy(g, d).start()

        @pl.when(t >= LAG_DOWN)
        def _():
            g = t - LAG_DOWN
            p = g // steps
            s, w = lax.rem(g, SLOTS), lax.rem(g, DSLOTS)
            for d in range(n_y):
                hc_wait(g, d)
            d_copy(g).wait()
            acc[p] += jnp.dot(hid[s].reshape(rows, CHUNK), wd[w], preferred_element_type=jnp.float32)
            core_copy(g).wait_send()
            for d in range(1, n_y):
                y_copy(g, d).wait_send()
                hy_copy(g, d).wait_send()
            for d in range(n_y):
                hc_copy(g, d).wait_send()

            @pl.when(g + DSLOTS < total)
            def _():
                d_copy(g + DSLOTS).start()

            for pp in range(PASSES):
                @pl.when(g == pp * steps + steps - 1)
                def _():
                    evens = range(pp * per, (pp + 1) * per, 2)
                    for k in range(PIECES):
                        for q in evens:
                            m = (q + 1 - pp * per) * rb
                            out_snd[q + 1, k] = acc[pp, m:m + rb, k * wp:(k + 1) * wp].astype(jnp.bfloat16)
                            mid_copy(q + 1, k).start()
                    for k in range(PIECES):
                        for q in evens:
                            if q:
                                m = (q - pp * per) * rb
                                mid_copy(q + 1, k).wait_recv()
                                out_snd[q, k] = (acc[pp, m:m + rb, k * wp:(k + 1) * wp]
                                                 + out_mid[q // 2, k].astype(jnp.float32)).astype(jnp.bfloat16)
                                out_copy(q, k).start()
        return carry

    lax.fori_loop(0, total + LAG_DOWN, step, 0)

    for k in range(PIECES):
        mid_copy(1, k).wait_recv()
        res = acc[0, 0:rb, k * wp:(k + 1) * wp] + out_mid[0, k].astype(jnp.float32)
        for q in range(2, n_bulk, 2):
            out_copy(q, k).wait_recv()
            res = res + out_rcv[q // 2, k].astype(jnp.float32)
        out[:, k * wp:(k + 1) * wp] = res.astype(out.dtype)
    for q in range(1, n_bulk):
        tok_copy(q).wait_send()
    for k in range(PIECES):
        for q in range(0, n_bulk, 2):
            mid_copy(q + 1, k).wait_send()
            if q:
                out_copy(q, k).wait_send()


def body(n_loop, n_bulk, tokens, gate_weight, up_weight, down_weight):
    rb, dl = tokens.shape
    ff, dout = down_weight.shape
    n_y = n_loop // 2
    rows = n_bulk // PASSES * rb
    half = rows // 2
    r = half // n_y
    bf, f32 = jnp.bfloat16, jnp.float32
    dma = pltpu.SemaphoreType.DMA
    vmem = pl.BlockSpec(memory_space=pltpu.VMEM)
    hbm = pl.BlockSpec(memory_space=pl.ANY)
    ny1 = max(n_y - 1, 1)
    return pl.pallas_call(
        functools.partial(kernel, n_loop, n_bulk),
        out_shape=jax.ShapeDtypeStruct((rb, dout), bf),
        in_specs=[vmem, hbm, hbm, hbm],
        out_specs=vmem,
        scratch_shapes=[
            pltpu.VMEM((n_bulk, rb, dl), bf),
            pltpu.VMEM((WSLOTS, dl, CHUNK), bf),
            pltpu.VMEM((WSLOTS, dl, CHUNK), bf),
            pltpu.VMEM((DSLOTS, CHUNK, dout), bf),
            pltpu.VMEM((SLOTS, 2, half, 2 * CHUNK), bf),
            pltpu.VMEM((SLOTS, half, 2 * CHUNK), bf),
            pltpu.VMEM((SLOTS, n_y, r, 2 * CHUNK), bf),
            pltpu.VMEM((SLOTS, ny1, r, 2 * CHUNK), bf),
            pltpu.VMEM((SLOTS, 2, n_y, r, CHUNK), bf),
            pltpu.VMEM((PASSES, rows, dout), f32),
            pltpu.VMEM((n_bulk, PIECES, rb, dout // PIECES), bf),
            pltpu.VMEM((n_bulk // 2, PIECES, rb, dout // PIECES), bf),
            pltpu.VMEM((n_bulk // 2, PIECES, rb, dout // PIECES), bf),
            dma((WSLOTS,)), dma((WSLOTS,)), dma((DSLOTS,)),
            dma((n_bulk,)), dma((n_bulk,)),
            dma((SLOTS,)), dma((SLOTS,)),
            dma((SLOTS, ny1)), dma((SLOTS, ny1)),
            dma((SLOTS, ny1)), dma((SLOTS, ny1)),
            dma((SLOTS, n_y)), dma((SLOTS, n_y)),
            dma((n_bulk // 2, PIECES)), dma((n_bulk // 2, PIECES)),
            dma((n_bulk // 2, PIECES)), dma((n_bulk // 2, PIECES)),
        ],
        compiler_params=pltpu.CompilerParams(
            collective_id=0, has_side_effects=True, vmem_limit_bytes=58 * 1024 * 1024),
    )(tokens, gate_weight, up_weight, down_weight)


def solution(mesh):
    return jax.shard_map(
        functools.partial(body, mesh.shape["loop"], mesh.shape["bulk"]),
        mesh=mesh,
        in_specs=(
            P(("groups", "bulk"), "loop"),
            P("loop", "bulk"),
            P("loop", "bulk"),
            P("bulk", "loop"),
        ),
        out_specs=P(("groups", "bulk"), "loop"),
        check_vma=False,
    )
```

```python
import functools

import jax
import jax.numpy as jnp
from jax import lax
from jax.experimental import pallas as pl
from jax.experimental.pallas import tpu as pltpu
from jax.sharding import PartitionSpec as P

MESH = pl.DeviceIdType.MESH
PASSES = 2
CHUNKS = (512, 256, 128)
SLOTS = 16
WSLOTS = 4
DSLOTS = 4
PIECES = 4
LAGS = (1, 4, 7, 8)
LAG_SUM, LAG_HID, LAG_FWD, LAG_DOWN = LAGS


def width(ff):
    return next(c for c in CHUNKS if ff % c == 0)


def flip(b, r):
    out, k = b, 1
    while k <= r:
        if r & k:
            out = out + k * (1 - 2 * ((b // k) % 2))
        k *= 2
    return out


def kernel(n_loop, n_bulk, tok, gate_hbm, up_hbm, down_hbm, out,
           x, wg, wu, wd, part, core_rcv, ysum, y_rcv, hid, acc, out_snd, out_mid, out_rcv,
           wg_sem, wu_sem, wd_sem, tok_send, tok_recv, core_send, core_recv,
           y_send, y_recv, hy_send, hy_recv, hc_send, hc_recv, mid_send, mid_recv, out_send, out_recv):
    n_y = n_loop // 2
    rb, dl = tok.shape
    ff = gate_hbm.shape[1]
    chunk = width(ff)
    dout = down_hbm.shape[1]
    wp = dout // PIECES
    steps = ff // chunk
    total = PASSES * steps
    per = n_bulk // PASSES
    rows = per * rb
    half = rows // 2
    r = half // n_y

    l = lax.axis_index("loop")
    b = lax.axis_index("bulk")
    y, c = l // 2, l % 2
    sib = y * 2 + (1 - c)
    oc = 1 - c

    def y_to(d):
        return lax.rem(y + d, n_y)

    def y_from(d):
        return lax.rem(y + n_y - d, n_y)

    def gu_copies(g):
        s = lax.rem(g, WSLOTS)
        col = pl.multiple_of(lax.rem(g, steps) * chunk, chunk)
        return (pltpu.make_async_copy(gate_hbm.at[:, pl.ds(col, chunk)], wg.at[s], wg_sem.at[s]),
                pltpu.make_async_copy(up_hbm.at[:, pl.ds(col, chunk)], wu.at[s], wu_sem.at[s]))

    def d_copy(g):
        s = lax.rem(g, DSLOTS)
        row = pl.multiple_of(lax.rem(g, steps) * chunk, chunk)
        return pltpu.make_async_copy(down_hbm.at[pl.ds(row, chunk), :], wd.at[s], wd_sem.at[s])

    for g in range(min(WSLOTS, total)):
        for cp in gu_copies(jnp.int32(g)):
            cp.start()
    for g in range(min(DSLOTS, total)):
        d_copy(jnp.int32(g)).start()

    barrier = pltpu.get_barrier_semaphore()
    pl.semaphore_signal(barrier, inc=1, device_id={"loop": sib}, device_id_type=MESH)
    for d in range(1, n_y):
        pl.semaphore_signal(barrier, inc=1, device_id={"loop": y_to(d) * 2 + c}, device_id_type=MESH)
    for q in range(1, n_bulk):
        pl.semaphore_signal(barrier, inc=1, device_id={"bulk": flip(b, q)}, device_id_type=MESH)
    pl.semaphore_wait(barrier, 1 + (n_y - 1) + (n_bulk - 1))

    def tok_copy(q):
        return pltpu.make_async_remote_copy(
            src_ref=tok, dst_ref=x.at[q], send_sem=tok_send.at[q], recv_sem=tok_recv.at[q],
            device_id={"bulk": flip(b, q)}, device_id_type=MESH)

    def core_copy(g):
        s = lax.rem(g, SLOTS)
        return pltpu.make_async_remote_copy(
            src_ref=part.at[s, oc], dst_ref=core_rcv.at[s], send_sem=core_send.at[s],
            recv_sem=core_recv.at[s], device_id={"loop": sib}, device_id_type=MESH)

    def y_copy(g, d):
        s = lax.rem(g, SLOTS)
        return pltpu.make_async_remote_copy(
            src_ref=ysum.at[s, y_to(d)], dst_ref=y_rcv.at[s, d - 1], send_sem=y_send.at[s, d - 1],
            recv_sem=y_recv.at[s, d - 1], device_id={"loop": y_to(d) * 2 + c}, device_id_type=MESH)

    def hy_copy(g, d):
        s = lax.rem(g, SLOTS)
        return pltpu.make_async_remote_copy(
            src_ref=hid.at[s, c, y], dst_ref=hid.at[s, c, y], send_sem=hy_send.at[s, d - 1],
            recv_sem=hy_recv.at[s, d - 1], device_id={"loop": y_to(d) * 2 + c}, device_id_type=MESH)

    def hy_wait(g, d):
        s = lax.rem(g, SLOTS)
        pltpu.make_async_remote_copy(
            src_ref=hid.at[s, c, y], dst_ref=hid.at[s, c, y_from(d)], send_sem=hy_send.at[s, d - 1],
            recv_sem=hy_recv.at[s, d - 1], device_id={"loop": y_to(d) * 2 + c},
            device_id_type=MESH).wait_recv()

    def hc_copy(g, d):
        s = lax.rem(g, SLOTS)
        return pltpu.make_async_remote_copy(
            src_ref=hid.at[s, c, y_from(d)], dst_ref=hid.at[s, c, y_from(d)], send_sem=hc_send.at[s, d],
            recv_sem=hc_recv.at[s, d], device_id={"loop": sib}, device_id_type=MESH)

    def hc_wait(g, d):
        s = lax.rem(g, SLOTS)
        pltpu.make_async_remote_copy(
            src_ref=hid.at[s, c, y_from(d)], dst_ref=hid.at[s, oc, y_from(d)], send_sem=hc_send.at[s, d],
            recv_sem=hc_recv.at[s, d], device_id={"loop": sib}, device_id_type=MESH).wait_recv()

    def mid_copy(q, k):
        return pltpu.make_async_remote_copy(
            src_ref=out_snd.at[q, k], dst_ref=out_mid.at[q // 2, k], send_sem=mid_send.at[q // 2, k],
            recv_sem=mid_recv.at[q // 2, k], device_id={"bulk": flip(b, 1)}, device_id_type=MESH)

    def out_copy(q, k):
        return pltpu.make_async_remote_copy(
            src_ref=out_snd.at[q, k], dst_ref=out_rcv.at[q // 2, k], send_sem=out_send.at[q // 2, k],
            recv_sem=out_recv.at[q // 2, k], device_id={"bulk": flip(b, q)}, device_id_type=MESH)

    for q in range(1, per):
        tok_copy(q).start()
    x[0] = tok[...]
    acc[...] = jnp.zeros_like(acc)
    for q in range(1, per):
        tok_copy(q).wait_recv()
    for q in range(max(per, 1), n_bulk):
        tok_copy(q).start()

    def step(t, carry):
        @pl.when(t < total)
        def _():
            g = t
            p = g // steps
            s, w = lax.rem(g, SLOTS), lax.rem(g, WSLOTS)
            for pp in range(1, PASSES):
                @pl.when(g == pp * steps)
                def _():
                    for q in range(pp * per, (pp + 1) * per):
                        tok_copy(q).wait_recv()
            for cp in gu_copies(g):
                cp.wait()
            rows_x = x[pl.ds(p * per, per)].reshape(rows, dl)
            gp = jnp.dot(rows_x, wg[w], preferred_element_type=jnp.float32)
            part[s, :, :, :chunk] = gp.astype(jnp.bfloat16).reshape(2, half, chunk)
            up = jnp.dot(rows_x, wu[w], preferred_element_type=jnp.float32)
            part[s, :, :, chunk:] = up.astype(jnp.bfloat16).reshape(2, half, chunk)
            core_copy(g).start()

            @pl.when(g + WSLOTS < total)
            def _():
                for cp in gu_copies(g + WSLOTS):
                    cp.start()

        @pl.when((t >= LAG_SUM) & (t < total + LAG_SUM))
        def _():
            g = t - LAG_SUM
            s = lax.rem(g, SLOTS)
            core_copy(g).wait_recv()
            both = part[s, c].astype(jnp.float32) + core_rcv[s].astype(jnp.float32)
            ysum[s] = both.astype(jnp.bfloat16).reshape(n_y, r, 2 * chunk)
            for d in range(1, n_y):
                y_copy(g, d).start()

        @pl.when((t >= LAG_HID) & (t < total + LAG_HID))
        def _():
            g = t - LAG_HID
            s = lax.rem(g, SLOTS)
            tot = ysum[s, y].astype(jnp.float32)
            for d in range(1, n_y):
                y_copy(g, d).wait_recv()
                tot = tot + y_rcv[s, d - 1].astype(jnp.float32)
            gate, up = tot[:, :chunk], tot[:, chunk:]
            hid[s, c, y] = (gate / (1.0 + jnp.exp(-gate)) * up).astype(jnp.bfloat16)
            for d in range(1, n_y):
                hy_copy(g, d).start()
            hc_copy(g, 0).start()

        @pl.when((t >= LAG_FWD) & (t < total + LAG_FWD))
        def _():
            g = t - LAG_FWD
            for d in range(1, n_y):
                hy_wait(g, d)
                hc_copy(g, d).start()

        @pl.when(t >= LAG_DOWN)
        def _():
            g = t - LAG_DOWN
            p = g // steps
            s, w = lax.rem(g, SLOTS), lax.rem(g, DSLOTS)
            for d in range(n_y):
                hc_wait(g, d)
            d_copy(g).wait()
            acc[p] += jnp.dot(hid[s].reshape(rows, chunk), wd[w], preferred_element_type=jnp.float32)
            core_copy(g).wait_send()
            for d in range(1, n_y):
                y_copy(g, d).wait_send()
                hy_copy(g, d).wait_send()
            for d in range(n_y):
                hc_copy(g, d).wait_send()

            @pl.when(g + DSLOTS < total)
            def _():
                d_copy(g + DSLOTS).start()

            for pp in range(PASSES):
                @pl.when(g == pp * steps + steps - 1)
                def _():
                    evens = range(pp * per, (pp + 1) * per, 2)
                    for k in range(PIECES):
                        for q in evens:
                            m = (q + 1 - pp * per) * rb
                            out_snd[q + 1, k] = acc[pp, m:m + rb, k * wp:(k + 1) * wp].astype(jnp.bfloat16)
                            mid_copy(q + 1, k).start()
                    for k in range(PIECES):
                        for q in evens:
                            if q:
                                m = (q - pp * per) * rb
                                mid_copy(q + 1, k).wait_recv()
                                out_snd[q, k] = (acc[pp, m:m + rb, k * wp:(k + 1) * wp]
                                                 + out_mid[q // 2, k].astype(jnp.float32)).astype(jnp.bfloat16)
                                out_copy(q, k).start()
        return carry

    lax.fori_loop(0, total + LAG_DOWN, step, 0)

    for k in range(PIECES):
        mid_copy(1, k).wait_recv()
        res = acc[0, 0:rb, k * wp:(k + 1) * wp] + out_mid[0, k].astype(jnp.float32)
        for q in range(2, n_bulk, 2):
            out_copy(q, k).wait_recv()
            res = res + out_rcv[q // 2, k].astype(jnp.float32)
        out[:, k * wp:(k + 1) * wp] = res.astype(out.dtype)
    for q in range(1, n_bulk):
        tok_copy(q).wait_send()
    for k in range(PIECES):
        for q in range(0, n_bulk, 2):
            mid_copy(q + 1, k).wait_send()
            if q:
                out_copy(q, k).wait_send()


def body(n_loop, n_bulk, tokens, gate_weight, up_weight, down_weight):
    rb, dl = tokens.shape
    ff, dout = down_weight.shape
    chunk = width(ff)
    n_y = n_loop // 2
    rows = n_bulk // PASSES * rb
    half = rows // 2
    r = half // n_y
    bf, f32 = jnp.bfloat16, jnp.float32
    dma = pltpu.SemaphoreType.DMA
    vmem = pl.BlockSpec(memory_space=pltpu.VMEM)
    hbm = pl.BlockSpec(memory_space=pl.ANY)
    ny1 = max(n_y - 1, 1)
    return pl.pallas_call(
        functools.partial(kernel, n_loop, n_bulk),
        out_shape=jax.ShapeDtypeStruct((rb, dout), bf),
        in_specs=[vmem, hbm, hbm, hbm],
        out_specs=vmem,
        scratch_shapes=[
            pltpu.VMEM((n_bulk, rb, dl), bf),
            pltpu.VMEM((WSLOTS, dl, chunk), bf),
            pltpu.VMEM((WSLOTS, dl, chunk), bf),
            pltpu.VMEM((DSLOTS, chunk, dout), bf),
            pltpu.VMEM((SLOTS, 2, half, 2 * chunk), bf),
            pltpu.VMEM((SLOTS, half, 2 * chunk), bf),
            pltpu.VMEM((SLOTS, n_y, r, 2 * chunk), bf),
            pltpu.VMEM((SLOTS, ny1, r, 2 * chunk), bf),
            pltpu.VMEM((SLOTS, 2, n_y, r, chunk), bf),
            pltpu.VMEM((PASSES, rows, dout), f32),
            pltpu.VMEM((n_bulk, PIECES, rb, dout // PIECES), bf),
            pltpu.VMEM((n_bulk // 2, PIECES, rb, dout // PIECES), bf),
            pltpu.VMEM((n_bulk // 2, PIECES, rb, dout // PIECES), bf),
            dma((WSLOTS,)), dma((WSLOTS,)), dma((DSLOTS,)),
            dma((n_bulk,)), dma((n_bulk,)),
            dma((SLOTS,)), dma((SLOTS,)),
            dma((SLOTS, ny1)), dma((SLOTS, ny1)),
            dma((SLOTS, ny1)), dma((SLOTS, ny1)),
            dma((SLOTS, n_y)), dma((SLOTS, n_y)),
            dma((n_bulk // 2, PIECES)), dma((n_bulk // 2, PIECES)),
            dma((n_bulk // 2, PIECES)), dma((n_bulk // 2, PIECES)),
        ],
        compiler_params=pltpu.CompilerParams(
            collective_id=0, has_side_effects=True, vmem_limit_bytes=58 * 1024 * 1024),
    )(tokens, gate_weight, up_weight, down_weight)


def solution(mesh):
    return jax.shard_map(
        functools.partial(body, mesh.shape["loop"], mesh.shape["bulk"]),
        mesh=mesh,
        in_specs=(
            P(("groups", "bulk"), "loop"),
            P("loop", "bulk"),
            P("loop", "bulk"),
            P("bulk", "loop"),
        ),
        out_specs=P(("groups", "bulk"), "loop"),
        check_vma=False,
    )
```
